512 devices in a mesh: enc: 2 (over y_lo), blk: 32 (over x, y_hi, core), uly: 8 (over z).
Axes of the slice: x: 4, y: 8 (y_hi: 4, y_lo: 2; y = y_hi * 2 + y_lo), z: 8, core: 2. Of those that a mesh axis runs over, the one named last changes fastest.
Arguments:
- img_query: bfloat16 [2, 14336, 2048], P('enc', ('blk', 'uly')), may hold values from -6 to 6
- img_key: bfloat16 [2, 14336, 2048], P('enc', ('blk', 'uly')), may hold values from -6 to 6
- img_value: bfloat16 [2, 14336, 2048], P('enc', ('blk', 'uly')), may hold values from -6 to 6
- text_query: bfloat16 [2, 256, 2048], P(None, ('blk', 'enc'), 'uly'), may hold values from -6 to 6
- text_key: bfloat16 [2, 256, 2048], P(None, ('blk', 'enc'), 'uly'), may hold values from -8 to 8
- text_value: bfloat16 [2, 256, 2048], P(None, ('blk', 'enc'), 'uly'), may hold values from -6 to 6
- text_len: int32 [2], P('enc'), may hold values from 85 to 256, as said below
Outputs:
- img_out: bfloat16 [2, 14336, 2048], P('enc', ('blk', 'uly'))
- text_out: bfloat16 [2, 256, 2048], P('enc', 'blk', 'uly')
The draws below stay inside these ranges and needn't reach their ends.
Inputs may be any that keep to these rules, and one draw needn't show every extreme that they name: `text_len`: one prompt uses all 256 rows, the other 85 or more.
All inputs are finite; a program needn't handle non-finite values.
Results may differ from the reference program's by a relative error of at most 0.007.
Values may be sent and summed in bfloat16 or wider, within the bound.
No kernel may reach another device: no remote copies, remote signals or barrier semaphores. Data moves between devices by JAX's collectives and lax.ppermute only.
A program may use at most 192 MiB of HBM per device.

```python
import math
import jax
import jax.numpy as jnp
from jax import lax

HD = 128
HEADS = 16
BATCH = 2
TEXT = 256
S_IMG = 14336


def draw_img_query(key, part):
    key = jax.random.fold_in(key, 1)
    entries = jnp.clip(1.7 * jax.random.normal(key, (BATCH, S_IMG, HEADS * HD), jnp.float32), -6.0, 6.0)
    return entries.astype(jnp.bfloat16)


def draw_img_key(key, part):
    key = jax.random.fold_in(key, 2)
    entries = jnp.clip(1.7 * jax.random.normal(key, (BATCH, S_IMG, HEADS * HD), jnp.float32), -6.0, 6.0)
    return entries.astype(jnp.bfloat16)


def draw_text_query(key, part):
    key = jax.random.fold_in(key, 3)
    entries = jnp.clip(1.7 * jax.random.normal(key, (BATCH, TEXT, HEADS * HD), jnp.float32), -6.0, 6.0)
    return entries.astype(jnp.bfloat16)


def draw_text_key(key, part):
    key = jax.random.fold_in(key, 4)
    entries = jnp.clip(2.3 * jax.random.normal(key, (BATCH, TEXT, HEADS * HD), jnp.float32), -8.0, 8.0)
    return entries.astype(jnp.bfloat16)


def draw_text_len(key, part):
    key = jax.random.fold_in(key, 5)
    full_prompt = jax.random.randint(jax.random.fold_in(key, 1), (), 0, BATCH)
    others = jax.random.randint(jax.random.fold_in(key, 2), (BATCH,), TEXT // 3, TEXT + 1)
    lengths = jnp.where(jnp.arange(BATCH) == full_prompt, TEXT, others)
    return lengths.astype(jnp.int32)


def block_levels(rng, shape, pieces, smallest, high):
    def one(position, blocks):
        draws = jax.random.uniform(jax.random.fold_in(jax.random.fold_in(rng, 6), position), (blocks,), jnp.float32, smallest / len(pieces), high / len(pieces))
        return jnp.repeat(jnp.exp(draws), shape[position] // blocks).reshape((-1,) + (1,) * (len(shape) - position - 1))

    loudness = one(*pieces[0])
    for cut in pieces[1:]:
        loudness = loudness * one(*cut)
    return loudness


def centred(own_key, extent, deviation, reach, cuts=(), kind=jnp.bfloat16):
    level = block_levels(own_key, extent, cuts, -0.22, 0.18) if cuts else 1.0
    values = jax.random.normal(own_key, extent, jnp.float32) * deviation * level
    return jnp.minimum(jnp.maximum(values, -reach), reach).astype(kind)


def setup_inputs(seed: int = 0) -> dict:
    seeds = jax.random.split(jax.random.key(seed), 8)
    return {
        "img_query": draw_img_query(jax.random.fold_in(seeds[7], 71), 0),
        "img_key": draw_img_key(jax.random.fold_in(seeds[7], 71), 0),
        "img_value": centred(seeds[2], (BATCH, S_IMG, HEADS * HD), 1.0, 6.0, ((0, 2), (1, 256))),
        "text_query": draw_text_query(jax.random.fold_in(seeds[7], 71), 0),
        "text_key": draw_text_key(jax.random.fold_in(seeds[7], 71), 0),
        "text_value": centred(seeds[5], (BATCH, TEXT, HEADS * HD), 1.0, 6.0, ((1, 64), (2, 8))),
        "text_len": draw_text_len(jax.random.fold_in(seeds[7], 71), 0),
    }


def attend(queries, key_rows, values, key_valid, score_scale):
    scores = jnp.dot(queries, key_rows.T, preferred_element_type=jnp.float32) * score_scale
    scores = jnp.where(key_valid[None, :], scores, -1e30)
    row_max = jnp.max(scores, axis=1, keepdims=True)
    weights = jnp.where(key_valid[None, :], jnp.exp(scores - row_max), 0.0)
    denominator = jnp.sum(weights, axis=1, keepdims=True)
    numerator = jnp.dot(weights.astype(jnp.bfloat16), values, preferred_element_type=jnp.float32)
    return (numerator / denominator).astype(jnp.bfloat16)


def reference(img_query, img_key, img_value, text_query, text_key, text_value, text_len):
    score_scale = HD ** -0.5
    query_block = math.gcd(S_IMG, 512)
    image_list = []
    text_list = []
    for prompt in range(BATCH):
        all_keys = jnp.concatenate([img_key[prompt], text_key[prompt]], 0)
        all_keys = all_keys.reshape(S_IMG + TEXT, HEADS, HD).transpose(1, 0, 2)
        all_values = jnp.concatenate([img_value[prompt], text_value[prompt]], 0)
        all_values = all_values.reshape(S_IMG + TEXT, HEADS, HD).transpose(1, 0, 2)
        text_index = jnp.arange(TEXT).astype(jnp.int32)
        key_valid = jnp.concatenate([jnp.ones((S_IMG,), dtype=bool), text_index < text_len[prompt].astype(jnp.int32)])
        image_queries = img_query[prompt].reshape(S_IMG // query_block, query_block, HEADS, HD).transpose(2, 0, 1, 3)
        text_queries = text_query[prompt].reshape(TEXT, HEADS, HD).transpose(1, 0, 2)

        def per_head(head_items):
            head_queries, head_text, head_keys, head_values = head_items
            image_part = lax.map(lambda row_block: attend(row_block, head_keys, head_values, key_valid, score_scale), head_queries)
            text_part = attend(head_text, head_keys, head_values, key_valid, score_scale)
            return image_part, text_part

        image_out, text_out = lax.map(per_head, (image_queries, text_queries, all_keys, all_values))
        image_list.append(image_out.transpose(1, 2, 0, 3).reshape(S_IMG, HEADS * HD))
        text_list.append(text_out.transpose(1, 0, 2).reshape(TEXT, HEADS * HD))
    return jnp.stack(image_list, 0), jnp.stack(text_list, 0)
```

```python
import jax
import jax.numpy as jnp
import numpy as np
from jax import lax
from jax.experimental import pallas as pl
from jax.experimental.pallas import tpu as pltpu
from jax.sharding import Mesh, PartitionSpec as P

HD = 128
HEADS = 16
ROWS = 56
TROWS = 8
GROUP = ROWS + TROWS
IMG = HEADS * ROWS
TXT = 4 * TROWS
BLOCK = IMG + TXT
LOG2_SCALE = float(HD ** -0.5 * np.log2(np.e))
MASKED = -1e30
AXES = ("enc", "x", "ya", "yb", "core", "za", "zb")
HEAD_AXES = ("za", "ya", "yb")
BF16, F32 = jnp.bfloat16, jnp.float32

VMEM = pl.BlockSpec(memory_space=pltpu.VMEM)
SMEM = pl.BlockSpec(memory_space=pltpu.SMEM)


def call(kernel, outs, args, name, flops=0, scratch=(), limit=48):
    size = sum(int(np.prod(a.shape)) * a.dtype.itemsize for a in args)
    size += sum(int(np.prod(o.shape)) * o.dtype.itemsize for o in outs)
    return pl.pallas_call(
        kernel,
        in_specs=[SMEM if a.dtype == jnp.int32 else VMEM for a in args],
        out_specs=[VMEM] * len(outs),
        out_shape=outs,
        scratch_shapes=list(scratch),
        compiler_params=pltpu.CompilerParams(vmem_limit_bytes=limit * 2**20),
        cost_estimate=pl.CostEstimate(flops=flops, bytes_accessed=size, transcendentals=0),
        name=name,
    )(*args)


def pack_kernel(place, text, query, key, value, out):
    z = place[0]
    for head in range(HEADS):
        here = (z == head // 2).astype(F32)
        columns = slice(head * HD, (head + 1) * HD)
        half = slice((head % 2) * HD, (head % 2 + 1) * HD)
        for part, rows in enumerate((query, key, value)):
            both = jnp.concatenate(
                [rows[0, :, columns].astype(F32), text[part, :, half].astype(F32) * here], 0
            )
            out[head, part * GROUP : (part + 1) * GROUP, :] = both.astype(BF16)


def unpack_kernel(place, chunks, query, kv):
    za = place[0]
    for part in range(3):
        dest = query if part == 0 else kv.at[part - 1]
        rows = slice(part * GROUP, (part + 1) * GROUP)
        for pair in range(HEADS // 2):
            two = [chunks[2 * pair + i, rows, :].astype(F32)[:ROWS] for i in range(2)]
            dest[2 * ROWS * pair : 2 * ROWS * (pair + 1), :] = jnp.concatenate(two, 0).astype(BF16)
        text = [chunks[4 * za + y, rows, :].astype(F32)[ROWS:] for y in range(4)]
        dest[IMG:BLOCK, :] = jnp.concatenate(text, 0).astype(BF16)


def flash_kernel(place, query, kv0, kv1, kv2, kv3, out, lse, text_k, text_v):
    tile = BLOCK // 2
    x, has_text, text_len = place[0], place[1], place[2]
    blocks = [(kv, core) for kv in (kv0, kv1, kv2, kv3) for core in range(2)]
    for i, (kv, core) in enumerate(blocks):
        text_k[TXT * i : TXT * (i + 1), :] = kv[core, 0, IMG:BLOCK, :]
        text_v[TXT * i : TXT * (i + 1), :] = kv[core, 1, IMG:BLOCK, :]
    column = lax.broadcasted_iota(jnp.int32, (1, TXT * len(blocks)), 1)
    from_x = (x - (column >> 6)) & 3
    index = (((from_x * 4 + ((column >> 3) & 3)) * 2 + ((column >> 5) & 1)) << 3) + (column & 7)
    limit = jnp.where(has_text > 0, text_len, 0)
    bias = jnp.where(index < limit, 0.0, MASKED)

    keys = [lambda kv=kv, core=core: kv[core, 0, :IMG, :] for kv, core in blocks] + [lambda: text_k[...]]
    values = [lambda kv=kv, core=core: kv[core, 1, :IMG, :] for kv, core in blocks] + [lambda: text_v[...]]

    def one_tile(step, carry):
        rows = pl.ds(pl.multiple_of(step * tile, 16), tile)
        q = query[rows, :]

        def score(i):
            return lax.dot_general(
                q, keys[i](), (((1,), (1,)), ((), ())), preferred_element_type=F32
            )

        top = jnp.full((tile, 1), MASKED, F32)
        both = jnp.zeros((tile, 2 * HD), F32)
        later = score(0)
        for i in range(len(keys)):
            s = later
            if i + 1 < len(keys):
                later = score(i + 1)
            if i == len(blocks):
                s = s + bias
            new_top = jnp.maximum(top, jnp.max(s, axis=1, keepdims=True))
            rescale = jnp.exp2((top - new_top) * LOG2_SCALE)
            weights = jnp.exp2((s - new_top) * LOG2_SCALE)
            v = values[i]()
            v = jnp.concatenate([v, jnp.ones(v.shape, BF16)], 1)
            both = both * rescale + jnp.dot(weights.astype(BF16), v, preferred_element_type=F32)
            top = new_top
        total = both[:, HD : HD + 1]
        out[rows, :] = (both[:, :HD] / total).astype(out.dtype)
        lse[rows, :] = jnp.broadcast_to(top * LOG2_SCALE + jnp.log2(total), (tile, HD))
        return carry

    lax.fori_loop(0, 2, one_tile, 0)


def lse_kernel(lse, out):
    out[...] = lse[...].T[:8]


def merge_kernel(place, out_a, lse_a, out_b, lse_b, chunks):
    za = place[0]
    a = lse_a[...]
    b = jnp.broadcast_to(lse_b[0:1, :], (HD, BLOCK)).T
    top = jnp.maximum(a, b)
    weight_a, weight_b = jnp.exp2(a - top), jnp.exp2(b - top)
    merged = (out_a[...] * weight_a + out_b[...].astype(F32) * weight_b) / (weight_a + weight_b)
    for source in range(HEADS):
        y = source % 4
        here = (za == source // 4).astype(F32)
        rows = [merged[ROWS * source : ROWS * (source + 1)], merged[IMG + TROWS * y : IMG + TROWS * (y + 1)] * here]
        chunks[source, :, :] = jnp.concatenate(rows, 0).astype(BF16)


def spread_kernel(place, chunks, img, text):
    z = place[0]
    for head in range(HEADS):
        img[0, :, head * HD : (head + 1) * HD] = chunks[head, :, :].astype(F32)[:ROWS].astype(BF16)
    for half in range(2):
        text[0, :, half * HD : (half + 1) * HD] = chunks[2 * z + half, :, :].astype(F32)[ROWS:].astype(BF16)


def shape(*dims, dtype=BF16):
    return jax.ShapeDtypeStruct(dims, dtype)


def shift(rows, axis, by):
    n = lax.axis_size(axis)
    return lax.ppermute(rows, axis, [(i, (i + by) % n) for i in range(n)])


def local(img_query, img_key, img_value, text_query, text_key, text_value, text_len):
    enc, x = lax.axis_index("enc"), lax.axis_index("x")
    za, zb = lax.axis_index("za"), lax.axis_index("zb")
    yh = lax.axis_index(("ya", "yb"))
    z = za * 2 + zb

    def scalars(*values):
        return jnp.stack([jnp.asarray(v, jnp.int32) for v in values])

    texts = jnp.stack([text_query, text_key, text_value])
    mine = lax.dynamic_index_in_dim(texts, enc, 1, keepdims=False)
    away = lax.dynamic_index_in_dim(texts, 1 - enc, 1, keepdims=False)
    got = shift(away, "enc", 1)
    text = jnp.where(
        enc == 0, jnp.concatenate([mine, got], 1), jnp.concatenate([got, mine], 1)
    )
    (chunks,) = call(
        pack_kernel,
        [shape(HEADS, 3 * GROUP, HD)],
        [scalars(z), text, img_query, img_key, img_value],
        "pack",
    )
    chunks = lax.all_to_all(chunks, HEAD_AXES, 0, 0, tiled=True)
    query, kv = call(
        unpack_kernel, [shape(BLOCK, HD), shape(2, BLOCK, HD)], [scalars(za), chunks], "unpack"
    )
    kvs = [kv, shift(kv, "x", 1), shift(kv, "x", 2), shift(kv, "x", -1)]
    other = shift(query, "zb", 1)
    kvs = [lax.all_gather(one, "core") for one in kvs]

    place = scalars(x, (zb == yh // 2), text_len[0])

    def flash(rows, dtype, name):
        return call(
            flash_kernel,
            [shape(BLOCK, HD, dtype=dtype), shape(BLOCK, HD, dtype=F32)],
            [place, rows, *kvs],
            name,
            flops=4 * BLOCK * 8 * BLOCK * HD,
            scratch=[pltpu.VMEM((8 * TXT, HD), BF16)] * 2,
        )

    away_out, away_lse = flash(other, BF16, "flash_other")
    (away_lse,) = call(lse_kernel, [shape(8, BLOCK, dtype=F32)], [away_lse], "lse")
    got_out, got_lse = shift(away_out, "zb", 1), shift(away_lse, "zb", 1)
    own_out, own_lse = flash(query, F32, "flash_own")
    (chunks,) = call(
        merge_kernel,
        [shape(HEADS, GROUP, HD)],
        [scalars(za), own_out, own_lse, got_out, got_lse],
        "merge",
    )
    chunks = lax.all_to_all(chunks, HEAD_AXES, 0, 0, tiled=True)
    return tuple(
        call(spread_kernel, [shape(1, ROWS, HEADS * HD), shape(1, TROWS, 2 * HD)], [scalars(z), chunks], "spread")
    )


def solution(mesh):
    fine = Mesh(mesh.devices.reshape(2, 4, 2, 2, 2, 4, 2), AXES)
    img = P("enc", AXES[1:], None)
    text = P(None, ("x", "ya", "yb", "core", "enc"), ("za", "zb"))
    return jax.shard_map(
        local,
        mesh=fine,
        in_specs=(img, img, img, text, text, text, P("enc")),
        out_specs=(img, P("enc", ("x", "ya", "yb", "core"), ("za", "zb"))),
        check_vma=False,
    )
```

```python
import functools

import jax
import jax.numpy as jnp
import numpy as np
from jax import lax
from jax.experimental import pallas as pl
from jax.experimental.pallas import tpu as pltpu
from jax.sharding import Mesh, PartitionSpec as P

HD = 128
HEADS = 16
ROWS = 56
TROWS = 8
GROUP = ROWS + TROWS
IMG = HEADS * ROWS
TXT = 4 * TROWS
BLOCK = IMG + TXT
LOG2_SCALE = float(HD ** -0.5 * np.log2(np.e))
MASKED = -1e30
AXES = ("enc", "x", "ya", "yb", "core", "za", "zb")
HEAD_AXES = ("za", "ya", "yb")
BF16, F32 = jnp.bfloat16, jnp.float32

VMEM = pl.BlockSpec(memory_space=pltpu.VMEM)
SMEM = pl.BlockSpec(memory_space=pltpu.SMEM)


def call(kernel, outs, args, name, flops=0, scratch=(), limit=12):
    size = sum(int(np.prod(a.shape)) * a.dtype.itemsize for a in args)
    size += sum(int(np.prod(o.shape)) * o.dtype.itemsize for o in outs)
    return pl.pallas_call(
        kernel,
        in_specs=[SMEM if a.dtype == jnp.int32 else VMEM for a in args],
        out_specs=[VMEM] * len(outs),
        out_shape=outs,
        scratch_shapes=list(scratch),
        compiler_params=pltpu.CompilerParams(vmem_limit_bytes=limit * 2**20),
        cost_estimate=pl.CostEstimate(flops=flops, bytes_accessed=size, transcendentals=0),
        name=name,
    )(*args)


def pack_kernel(query, key, value, out):
    for head in range(HEADS):
        for part, rows in enumerate((query, key, value)):
            both = [rows[0, :, head * HD : (head + 1) * HD].astype(F32), jnp.zeros((TROWS, HD), F32)]
            out[head, part * GROUP : (part + 1) * GROUP, :] = jnp.concatenate(both, 0).astype(BF16)


def pack_text_kernel(place, text, chunks, out):
    z = place[0]
    out[...] = chunks[...]
    for half in range(2):
        for part in range(3):
            rows = slice(part * GROUP, (part + 1) * GROUP)
            both = [
                chunks[2 * z + half, rows, :].astype(F32)[:ROWS],
                text[part, :, half * HD : (half + 1) * HD].astype(F32),
            ]
            out[2 * z + half, rows, :] = jnp.concatenate(both, 0).astype(BF16)


def unpack_kernel(place, chunks, query, kv):
    za = place[0]
    for part in range(3):
        dest = query if part == 0 else kv.at[part - 1]
        rows = slice(part * GROUP, (part + 1) * GROUP)
        for pair in range(HEADS // 2):
            two = [chunks[2 * pair + i, rows, :].astype(F32)[:ROWS] for i in range(2)]
            dest[2 * ROWS * pair : 2 * ROWS * (pair + 1), :] = jnp.concatenate(two, 0).astype(BF16)
        text = [chunks[4 * za + y, rows, :].astype(F32)[ROWS:] for y in range(4)]
        dest[IMG:BLOCK, :] = jnp.concatenate(text, 0).astype(BF16)


def packed(out, logs):
    high = logs.astype(BF16).astype(F32)
    middle = (logs - high).astype(BF16).astype(F32)
    low = logs - high - middle
    row = lax.broadcasted_iota(jnp.int32, logs.shape, 0)
    logs = jnp.where(row == 0, high, jnp.where(row == 1, middle, low))
    return jnp.concatenate([out, logs], 0).astype(BF16)


def unpacked(both):
    parts = both[HD : HD + 16, :].astype(F32)
    return both[:HD, :].astype(F32), parts[0:1] + parts[1:2] + parts[2:3]


def flash_kernel(place, *refs, groups, own):
    queries, (near, far), refs = refs[:groups], refs[groups : groups + 2], refs[groups + 2 :]
    outs, (sums, tops) = refs[:-2], refs[-2:]
    x, text_near, text_len = place[0], place[1], place[2]
    blocks = [(kv, core) for kv in (near, far) for core in range(2)]
    column = lax.broadcasted_iota(jnp.int32, (1, IMG + 2 * TXT), 1) - IMG
    index = (((x * 4 + ((column >> 3) & 3)) * 2 + ((column >> 5) & 1)) << 3) + (column & 7)
    bias = jnp.where((column < 0) | (index < text_len), 0.0, MASKED)

    def rows_of(part, i):
        kv, core = blocks[i]
        rows = kv[core, part, :IMG, :]
        if i < len(blocks) - 1:
            return rows
        text = [
            jnp.where(text_near > 0, near[core, part, IMG:BLOCK, :], far[core, part, IMG:BLOCK, :])
            for core in range(2)
        ]
        return jnp.concatenate([rows] + text, 0)

    def score(q, i):
        return lax.dot_general(
            q, rows_of(0, i), (((1,), (1,)), ((), ())), preferred_element_type=F32
        )

    parts = 2 if groups == 1 else 1
    tile = BLOCK // parts
    work = [(group, i) for group in range(groups * parts) for i in range(len(blocks))]
    rows = [query[part * tile : (part + 1) * tile, :] for query in queries for part in range(parts)]
    later = score(rows[0], 0)
    for n, (group, i) in enumerate(work):
        if i == 0:
            top = jnp.full((tile, 1), MASKED, F32)
            both = jnp.zeros((tile, 2 * HD), F32)
        s = later
        if n + 1 < len(work):
            later = score(rows[work[n + 1][0]], work[n + 1][1])
        if i == len(blocks) - 1:
            s = s + bias
        new_top = jnp.maximum(top, jnp.max(s, axis=1, keepdims=True))
        rescale = jnp.exp2((top - new_top) * LOG2_SCALE)
        weights = jnp.exp2((s - new_top) * LOG2_SCALE)
        v = rows_of(1, i)
        v = jnp.concatenate([v, jnp.ones(v.shape, BF16)], 1)
        both = both * rescale + jnp.dot(weights.astype(BF16), v, preferred_element_type=F32)
        top = new_top
        if i < len(blocks) - 1:
            continue
        total = both[:, HD : HD + 1]
        group, part = divmod(group, parts)
        span = slice(part * tile, (part + 1) * tile)
        sums[group, span, :] = both[:, :HD] / total
        tops[group, span, :] = jnp.broadcast_to(top * LOG2_SCALE + jnp.log2(total), (tile, HD))
        if part < parts - 1:
            continue
        result, logs = sums[group].T, tops[group].T[:16]
        if own and group == groups - 1:
            outs[-2][...] = result
            outs[-1][...] = logs
        else:
            outs[group][...] = packed(result, logs)


def merge_kernel(place, own, own_log, got1, got2, got3, chunks):
    za = place[0]
    outs, logs = [own[...]], [own_log[:1]]
    for got in (got1, got2, got3):
        out, log = unpacked(got)
        outs.append(out)
        logs.append(log)
    top = jnp.maximum(jnp.maximum(logs[0], logs[1]), jnp.maximum(logs[2], logs[3]))
    weights = [jnp.exp2(log - top) for log in logs]
    total = weights[0] + weights[1] + weights[2] + weights[3]
    merged = sum(out * (weight / total) for out, weight in zip(outs, weights)).T
    for source in range(HEADS):
        y = source % 4
        here = (za == source // 4).astype(F32)
        rows = [merged[ROWS * source : ROWS * (source + 1)], merged[IMG + TROWS * y : IMG + TROWS * (y + 1)] * here]
        chunks[source, :, :] = jnp.concatenate(rows, 0).astype(BF16)


def spread_kernel(place, chunks, img, text):
    z = place[0]
    for head in range(HEADS):
        img[0, :, head * HD : (head + 1) * HD] = chunks[head, :, :].astype(F32)[:ROWS].astype(BF16)
    for half in range(2):
        text[0, :, half * HD : (half + 1) * HD] = chunks[2 * z + half, :, :].astype(F32)[ROWS:].astype(BF16)


def shape(*dims, dtype=BF16):
    return jax.ShapeDtypeStruct(dims, dtype)


def shift(rows, axis, by):
    n = lax.axis_size(axis)
    return lax.ppermute(rows, axis, [(i, (i + by) % n) for i in range(n)])


def local(img_query, img_key, img_value, text_query, text_key, text_value, text_len):
    enc, x = lax.axis_index("enc"), lax.axis_index("x")
    za, zb = lax.axis_index("za"), lax.axis_index("zb")
    yh = lax.axis_index(("ya", "yb"))
    z = za * 2 + zb

    def scalars(*values):
        return jnp.stack([jnp.asarray(v, jnp.int32) for v in values])

    texts = jnp.stack([text_query, text_key, text_value])
    mine = lax.dynamic_index_in_dim(texts, enc, 1, keepdims=False)
    away = lax.dynamic_index_in_dim(texts, 1 - enc, 1, keepdims=False)
    got = shift(away, "enc", 1)
    text = jnp.where(
        enc == 0, jnp.concatenate([mine, got], 1), jnp.concatenate([got, mine], 1)
    )
    (chunks,) = call(
        pack_kernel,
        [shape(HEADS, 3 * GROUP, HD)],
        [img_query, img_key, img_value],
        "pack",
    )
    (chunks,) = call(
        pack_text_kernel, [shape(HEADS, 3 * GROUP, HD)], [scalars(z), text, chunks], "pack_text"
    )
    chunks = lax.all_to_all(chunks, HEAD_AXES, 0, 0, tiled=True)
    query, kv = call(
        unpack_kernel, [shape(BLOCK, HD), shape(2, BLOCK, HD)], [scalars(za), chunks], "unpack"
    )
    far = shift(kv, "zb", 1)
    groups = [shift(query, "x", by) for by in (2, 1, -1)]
    near, far = lax.all_gather(kv, "core"), lax.all_gather(far, "core")
    place = scalars(x, (zb == yh // 2), text_len[0])

    def flash(name, rows, own=False):
        outs = [shape(HD + 16, BLOCK)] * (len(rows) - own)
        if own:
            outs += [shape(HD, BLOCK, dtype=F32), shape(16, BLOCK, dtype=F32)]
        return call(
            functools.partial(flash_kernel, groups=len(rows), own=own),
            outs,
            [place, *rows, near, far],
            name,
            flops=16 * len(rows) * BLOCK * BLOCK * HD,
            scratch=[pltpu.VMEM((len(rows), BLOCK, HD), F32)] * 2,
            limit=40,
        )

    away = flash("flash_two", groups[:2])
    got = [shift(rows, "x", by) for rows, by in zip(away, (-2, -1))]
    (away,) = flash("flash_third", groups[2:])
    got.append(shift(away, "x", 1))
    own, own_log = flash("flash_own", [query], own=True)
    (chunks,) = call(merge_kernel, [shape(HEADS, GROUP, HD)], [scalars(za), own, own_log, *got], "merge")
    chunks = lax.all_to_all(chunks, HEAD_AXES, 0, 0, tiled=True)
    return tuple(
        call(spread_kernel, [shape(1, ROWS, HEADS * HD), shape(1, TROWS, 2 * HD)], [scalars(z), chunks], "spread")
    )


def solution(mesh):
    fine = Mesh(mesh.devices.reshape(2, 4, 2, 2, 2, 4, 2), AXES)
    img = P("enc", AXES[1:], None)
    text = P(None, ("x", "ya", "yb", "core", "enc"), ("za", "zb"))
    return jax.shard_map(
        local,
        mesh=fine,
        in_specs=(img, img, img, text, text, text, P("enc")),
        out_specs=(img, P("enc", ("x", "ya", "yb", "core"), ("za", "zb"))),
        check_vma=False,
    )
```

```python
import functools

import jax
import jax.numpy as jnp
import numpy as np
from jax import lax
from jax.experimental import pallas as pl
from jax.experimental.pallas import tpu as pltpu
from jax.sharding import Mesh, PartitionSpec as P

HD = 128
HEADS = 16
ROWS = 56
TROWS = 8
GROUP = ROWS + TROWS
IMG = HEADS * ROWS
TXT = 4 * TROWS
BLOCK = IMG + TXT
LOG2_SCALE = float(HD ** -0.5 * np.log2(np.e))
MASKED = -1e30
AXES = ("enc", "x", "ya", "yb", "core", "za", "zb")
HEAD_AXES = ("za", "ya", "yb")
BF16, F32 = jnp.bfloat16, jnp.float32

VMEM = pl.BlockSpec(memory_space=pltpu.VMEM)
SMEM = pl.BlockSpec(memory_space=pltpu.SMEM)


def call(kernel, outs, args, name, flops=0, scratch=(), limit=12):
    size = sum(int(np.prod(a.shape)) * a.dtype.itemsize for a in args)
    size += sum(int(np.prod(o.shape)) * o.dtype.itemsize for o in outs)
    return pl.pallas_call(
        kernel,
        in_specs=[SMEM if a.dtype == jnp.int32 else VMEM for a in args],
        out_specs=[VMEM] * len(outs),
        out_shape=outs,
        scratch_shapes=list(scratch),
        compiler_params=pltpu.CompilerParams(vmem_limit_bytes=limit * 2**20),
        cost_estimate=pl.CostEstimate(flops=flops, bytes_accessed=size, transcendentals=0),
        name=name,
    )(*args)


def pack_kernel(query, key, value, out):
    for head in range(HEADS):
        for part, rows in enumerate((query, key, value)):
            both = [rows[0, :, head * HD : (head + 1) * HD].astype(F32), jnp.zeros((TROWS, HD), F32)]
            out[head, part * GROUP : (part + 1) * GROUP, :] = jnp.concatenate(both, 0).astype(BF16)


def pack_text_kernel(place, text, chunks, out):
    z = place[0]
    out[...] = chunks[...]
    for half in range(2):
        for part in range(3):
            rows = slice(part * GROUP, (part + 1) * GROUP)
            both = [
                chunks[2 * z + half, rows, :].astype(F32)[:ROWS],
                text[part, :, half * HD : (half + 1) * HD].astype(F32),
            ]
            out[2 * z + half, rows, :] = jnp.concatenate(both, 0).astype(BF16)


def unpack_kernel(place, chunks, query, kv):
    za = place[0]
    for part in range(3):
        dest = query if part == 0 else kv.at[part - 1]
        rows = slice(part * GROUP, (part + 1) * GROUP)
        for pair in range(HEADS // 2):
            two = [chunks[2 * pair + i, rows, :].astype(F32)[:ROWS] for i in range(2)]
            dest[2 * ROWS * pair : 2 * ROWS * (pair + 1), :] = jnp.concatenate(two, 0).astype(BF16)
        text = [chunks[4 * za + y, rows, :].astype(F32)[ROWS:] for y in range(4)]
        dest[IMG:BLOCK, :] = jnp.concatenate(text, 0).astype(BF16)


def packed(out, logs):
    high = logs.astype(BF16).astype(F32)
    middle = (logs - high).astype(BF16).astype(F32)
    low = logs - high - middle
    row = lax.broadcasted_iota(jnp.int32, logs.shape, 0)
    logs = jnp.where(row == 0, high, jnp.where(row == 1, middle, low))
    return jnp.concatenate([out, logs], 0).astype(BF16)


def unpacked(both):
    parts = both[HD : HD + 16, :].astype(F32)
    return both[:HD, :].astype(F32), parts[0:1] + parts[1:2] + parts[2:3]


def flash_kernel(place, *refs, groups, own):
    queries, (near, far), refs = refs[:groups], refs[groups : groups + 2], refs[groups + 2 :]
    outs, (sums, tops) = refs[:-2], refs[-2:]
    x, text_near, text_len = place[0], place[1], place[2]
    blocks = [(kv, core) for kv in (near, far) for core in range(2)]
    column = lax.broadcasted_iota(jnp.int32, (1, IMG + 2 * TXT), 1) - IMG
    index = (((x * 4 + ((column >> 3) & 3)) * 2 + ((column >> 5) & 1)) << 3) + (column & 7)
    bias = jnp.where((column < 0) | (index < text_len), 0.0, MASKED)

    def rows_of(part, i):
        kv, core = blocks[i]
        rows = kv[core, part, :IMG, :]
        if i < len(blocks) - 1:
            return rows
        text = [
            jnp.where(text_near > 0, near[core, part, IMG:BLOCK, :], far[core, part, IMG:BLOCK, :])
            for core in range(2)
        ]
        return jnp.concatenate([rows] + text, 0)

    def score(q, i):
        return lax.dot_general(
            q, rows_of(0, i), (((1,), (1,)), ((), ())), preferred_element_type=F32
        )

    parts = 2 if groups == 1 else 1
    tile = BLOCK // parts
    work = [(group, i) for group in range(groups * parts) for i in range(len(blocks))]
    rows = [query[part * tile : (part + 1) * tile, :] for query in queries for part in range(parts)]
    later = score(rows[0], 0)
    for n, (group, i) in enumerate(work):
        if i == 0:
            top = jnp.full((tile, 1), MASKED, F32)
            both = jnp.zeros((tile, 2 * HD), F32)
        s = later
        if n + 1 < len(work):
            later = score(rows[work[n + 1][0]], work[n + 1][1])
        if i == len(blocks) - 1:
            s = s + bias
        new_top = jnp.maximum(top, jnp.max(s, axis=1, keepdims=True))
        rescale = jnp.exp2((top - new_top) * LOG2_SCALE)
        weights = jnp.exp2((s - new_top) * LOG2_SCALE)
        v = rows_of(1, i)
        v = jnp.concatenate([v, jnp.ones(v.shape, BF16)], 1)
        both = both * rescale + jnp.dot(weights.astype(BF16), v, preferred_element_type=F32)
        top = new_top
        if i < len(blocks) - 1:
            continue
        total = both[:, HD : HD + 1]
        group, part = divmod(group, parts)
        span = slice(part * tile, (part + 1) * tile)
        sums[group, span, :] = both[:, :HD] / total
        tops[group, span, :] = jnp.broadcast_to(top * LOG2_SCALE + jnp.log2(total), (tile, HD))
        if part < parts - 1:
            continue
        result, logs = sums[group].T, tops[group].T[:16]
        if own and group == groups - 1:
            outs[-2][...] = result
            outs[-1][...] = logs
        else:
            outs[group][...] = packed(result, logs)


def merge_kernel(place, own, own_log, got1, got2, got3, chunks):
    za = place[0]
    outs, logs = [own[...]], [own_log[:1]]
    for got in (got1, got2, got3):
        out, log = unpacked(got)
        outs.append(out)
        logs.append(log)
    top = jnp.maximum(jnp.maximum(logs[0], logs[1]), jnp.maximum(logs[2], logs[3]))
    weights = [jnp.exp2(log - top) for log in logs]
    total = weights[0] + weights[1] + weights[2] + weights[3]
    merged = sum(out * (weight / total) for out, weight in zip(outs, weights)).T
    for source in range(HEADS):
        y = source % 4
        here = (za == source // 4).astype(F32)
        rows = [merged[ROWS * source : ROWS * (source + 1)], merged[IMG + TROWS * y : IMG + TROWS * (y + 1)] * here]
        chunks[source, :, :] = jnp.concatenate(rows, 0).astype(BF16)


def spread_kernel(place, chunks, img, text):
    z = place[0]
    for head in range(HEADS):
        img[0, :, head * HD : (head + 1) * HD] = chunks[head, :, :].astype(F32)[:ROWS].astype(BF16)
    for half in range(2):
        text[0, :, half * HD : (half + 1) * HD] = chunks[2 * z + half, :, :].astype(F32)[ROWS:].astype(BF16)


def shape(*dims, dtype=BF16):
    return jax.ShapeDtypeStruct(dims, dtype)


def shift(rows, axis, by):
    n = lax.axis_size(axis)
    return lax.ppermute(rows, axis, [(i, (i + by) % n) for i in range(n)])


def local(img_query, img_key, img_value, text_query, text_key, text_value, text_len):
    enc, x = lax.axis_index("enc"), lax.axis_index("x")
    za, zb = lax.axis_index("za"), lax.axis_index("zb")
    yh = lax.axis_index(("ya", "yb"))
    z = za * 2 + zb

    def scalars(*values):
        return jnp.stack([jnp.asarray(v, jnp.int32) for v in values])

    texts = jnp.stack([text_query, text_key, text_value])
    mine = lax.dynamic_index_in_dim(texts, enc, 1, keepdims=False)
    away = lax.dynamic_index_in_dim(texts, 1 - enc, 1, keepdims=False)
    got = shift(away, "enc", 1)
    text = jnp.where(
        enc == 0, jnp.concatenate([mine, got], 1), jnp.concatenate([got, mine], 1)
    )
    (chunks,) = call(
        pack_kernel,
        [shape(HEADS, 3 * GROUP, HD)],
        [img_query, img_key, img_value],
        "pack",
    )
    (chunks,) = call(
        pack_text_kernel, [shape(HEADS, 3 * GROUP, HD)], [scalars(z), text, chunks], "pack_text"
    )
    chunks = lax.all_to_all(chunks, HEAD_AXES, 0, 0, tiled=True)
    query, kv = call(
        unpack_kernel, [shape(BLOCK, HD), shape(2, BLOCK, HD)], [scalars(za), chunks], "unpack"
    )
    far = shift(kv, "zb", 1)
    groups = [shift(query, "x", by) for by in (1, -1, 2)]
    near, far = lax.all_gather(kv, "core"), lax.all_gather(far, "core")
    place = scalars(x, (zb == yh // 2), text_len[0])

    def flash(name, rows, own=False):
        outs = [shape(HD + 16, BLOCK)] * (len(rows) - own)
        if own:
            outs += [shape(HD, BLOCK, dtype=F32), shape(16, BLOCK, dtype=F32)]
        return call(
            functools.partial(flash_kernel, groups=len(rows), own=own),
            outs,
            [place, *rows, near, far],
            name,
            flops=16 * len(rows) * BLOCK * BLOCK * HD,
            scratch=[pltpu.VMEM((len(rows), BLOCK, HD), F32)] * 2,
            limit=40,
        )

    away = flash("flash_two", groups[:2])
    got = [shift(rows, "x", by) for rows, by in zip(away, (-1, 1))]
    (away,) = flash("flash_third", groups[2:])
    got.append(shift(away, "x", -2))
    own, own_log = flash("flash_own", [query], own=True)
    (chunks,) = call(merge_kernel, [shape(HEADS, GROUP, HD)], [scalars(za), own, own_log, *got], "merge")
    chunks = lax.all_to_all(chunks, HEAD_AXES, 0, 0, tiled=True)
    return tuple(
        call(spread_kernel, [shape(1, ROWS, HEADS * HD), shape(1, TROWS, 2 * HD)], [scalars(z), chunks], "spread")
    )


def solution(mesh):
    fine = Mesh(mesh.devices.reshape(2, 4, 2, 2, 2, 4, 2), AXES)
    img = P("enc", AXES[1:], None)
    text = P(None, ("x", "ya", "yb", "core", "enc"), ("za", "zb"))
    return jax.shard_map(
        local,
        mesh=fine,
        in_specs=(img, img, img, text, text, text, P("enc")),
        out_specs=(img, P("enc", ("x", "ya", "yb", "core"), ("za", "zb"))),
        check_vma=False,
    )
```
